512 devices in a mesh: ctx: 32 (over x_hi, z), head: 16 (over y, x_lo, core).
Axes of the slice: x: 4 (x_hi: 2, x_lo: 2; x = x_hi * 2 + x_lo), y: 4, z: 16, core: 2. Of those that a mesh axis runs over, the one named last changes fastest.
Arguments:
- queries: bfloat16 [4096, 12288], P('ctx', 'head'), may hold values from -400 to 400
- latents: bfloat16 [4096, 576], P('ctx'), may hold values from -1000 to 1000
- latent_gain: float32 [512], replicated, may hold values from 0.1 to 1.9
- latent_up: bfloat16 [512, 16384], P(None, 'head'), may hold values from -0.25 to 0.25
- out_weight: bfloat16 [8192, 7168], P('head', 'ctx'), may hold values from -0.75 to 0.75
- positions: int32 [4096], P('ctx'), may hold values from 0 to 4095, as said below
Outputs:
- mixed: bfloat16 [4096, 7168], P('ctx', 'head')
The draws below stay inside these ranges and needn't reach their ends.
Inputs may be any that keep to these rules, and one draw needn't show every extreme that they name: The rows of one device hold two runs of 64 consecutive positions, each rising and starting at a multiple of 64; over the whole sequence every position appears once.
All inputs are finite; a program needn't handle non-finite values.
Results may differ from the reference program's by a relative error of at most 0.024.
Values may be sent and summed in bfloat16 or wider, within the bound.
A program may use at most 64 MiB of HBM per device.

```python
import math
import jax
import jax.numpy as jnp
from jax import lax

D = 7168
HEADS = 64
NOPE = 128
ROPE = 64
VDIM = 128
LATENT = 512
TOKENS = 4096
BLOCK = 64


def shared_rope(key):
    return jax.random.normal(jax.random.fold_in(key, 11), (TOKENS, ROPE), jnp.float32)


def draw_latents(key, part):
    rope_part = shared_rope(key)
    key = jax.random.fold_in(key, 1)
    first_key, second_key, third_key = jax.random.split(key, 3)
    row_scale = jnp.exp(jax.random.uniform(first_key, (TOKENS, 1), jnp.float32) * math.log(10.0))
    column_scale = jnp.exp(jax.random.uniform(second_key, (1, LATENT), jnp.float32) * math.log(10.0))
    noise = jnp.clip(jax.random.normal(third_key, (TOKENS, LATENT), jnp.float32), -6.0, 6.0)
    return jnp.concatenate([noise * row_scale * column_scale, rope_part], axis=1).astype(jnp.bfloat16)


def draw_queries(key, part):
    key = jax.random.fold_in(key, 2)
    noise = jnp.clip(jax.random.normal(key, (TOKENS, HEADS, NOPE + ROPE), jnp.float32), -6.0, 6.0)
    return noise.reshape(TOKENS, HEADS * (NOPE + ROPE)).astype(jnp.bfloat16)


def draw_positions(key, part):
    key = jax.random.fold_in(key, 3)
    block_count = TOKENS // BLOCK
    order = jax.random.permutation(key, jnp.arange(block_count, dtype=jnp.int32))
    row_index = jnp.arange(TOKENS, dtype=jnp.int32)
    return (order[row_index // BLOCK] * BLOCK + row_index % BLOCK).astype(jnp.int32)


def level_of(own_key, shape, cuts, low, largest):
    def one(position, blocks):
        steps = jax.random.uniform(jax.random.fold_in(jax.random.fold_in(own_key, 6), position), (blocks,), jnp.float32, low / len(cuts), largest / len(cuts))
        return jnp.repeat(jnp.exp(steps), shape[position] // blocks).reshape((-1,) + (1,) * (len(shape) - position - 1))

    level = one(*cuts[0])
    for cut in cuts[1:]:
        level = level * one(*cut)
    return level


def bell_draw(key, extent, spread, reach, shards=(), held_as=jnp.bfloat16):
    array = spread * jax.random.normal(key, extent, jnp.float32)
    if shards:
        array = array * level_of(key, extent, shards, -0.22, 0.18)
    return jnp.clip(array, -reach, reach).astype(held_as)


def setup_inputs(seed: int = 0) -> dict:
    key_list = jax.random.split(jax.random.key(seed), 7)
    queries = draw_queries(jax.random.fold_in(key_list[6], 71), 0)
    latents = draw_latents(jax.random.fold_in(key_list[6], 71), 0)
    latent_gain = jnp.clip(1.0 + 0.18 * jax.random.normal(key_list[2], (LATENT,), jnp.float32), 0.1, 1.9)
    latent_up = bell_draw(key_list[3], (LATENT, HEADS * (NOPE + VDIM)), LATENT ** -0.5, 0.25, ((1, 16),))
    out_weight = bell_draw(key_list[4], (HEADS * VDIM, D), HEADS ** -0.5, 0.75, ((0, 16), (1, 32)))
    positions = draw_positions(jax.random.fold_in(key_list[6], 71), 0)
    return {"queries": queries, "latents": latents, "latent_gain": latent_gain, "latent_up": latent_up, "out_weight": out_weight, "positions": positions}


def rotate(values, angles):
    half_dim = values.shape[-1] // 2
    front_half = values[..., :half_dim]
    back_half = values[..., half_dim:]
    cosine = jnp.cos(angles)
    sine_part = jnp.sin(angles)
    return jnp.concatenate([front_half * cosine - back_half * sine_part, back_half * cosine + front_half * sine_part], axis=-1)

def angles_for(positions, width):
    half_dim = width // 2
    frequency = jnp.exp(jnp.arange(half_dim, dtype=jnp.float32) * (-2.0 * math.log(10000.0) / width))
    return positions.astype(jnp.float32)[:, None] * frequency[None, :]

def compress(latents, latent_gain, positions):
    nope_part = latents[:, :LATENT].astype(jnp.float32)
    mean_square = lax.optimization_barrier(jnp.mean(nope_part * nope_part, axis=-1, keepdims=True))
    normed = (nope_part * lax.rsqrt(mean_square + 1e-06) * latent_gain[None, :]).astype(jnp.bfloat16)
    angles = angles_for(positions, latents.shape[1] - LATENT)
    rotated = rotate(latents[:, LATENT:].astype(jnp.float32), angles).astype(jnp.bfloat16)
    return (normed, rotated, angles)

def reference(queries, latents, latent_gain, latent_up, out_weight, positions):
    normed, key_rope, angles = compress(latents, latent_gain, positions)
    grouped = queries.reshape(TOKENS, HEADS, NOPE + ROPE)
    query_nope = jnp.transpose(grouped[:, :, :NOPE], (1, 0, 2))
    query_rope = rotate(grouped[:, :, NOPE:].astype(jnp.float32), angles[:, None, :]).astype(jnp.bfloat16)
    query_rope = jnp.transpose(query_rope, (1, 0, 2))
    per_head = jnp.transpose(latent_up.reshape(LATENT, HEADS, NOPE + VDIM), (1, 0, 2))
    allowed = positions[None, :] <= positions[:, None]
    softmax_scale = (NOPE + ROPE) ** (-0.5)

    def attend(inputs):
        head_nope, head_rope, head_weights = inputs
        projected = jnp.dot(normed, head_weights, preferred_element_type=jnp.float32).astype(jnp.bfloat16)
        scores = jnp.dot(head_nope, projected[:, :NOPE].T, preferred_element_type=jnp.float32)
        scores = (scores + jnp.dot(head_rope, key_rope.T, preferred_element_type=jnp.float32)) * softmax_scale
        highest = lax.optimization_barrier(jnp.max(jnp.where(allowed, scores, -1e+30), axis=1, keepdims=True))
        exp_scores = jnp.where(allowed, jnp.exp(scores - highest), 0.0)
        totals = lax.optimization_barrier(jnp.sum(exp_scores, axis=1, keepdims=True))
        summed = jnp.dot(exp_scores.astype(jnp.bfloat16), projected[:, NOPE:], preferred_element_type=jnp.float32)
        return (summed / totals).astype(jnp.bfloat16)
    attended = lax.map(attend, (query_nope, query_rope, per_head))
    attended = jnp.transpose(attended, (1, 0, 2)).reshape(TOKENS, HEADS * VDIM)
    return jnp.dot(attended, out_weight, preferred_element_type=jnp.float32).astype(jnp.bfloat16)
```

```python
import math

import jax
import jax.numpy as jnp
from jax import lax
from jax.experimental import pallas as pl
from jax.experimental.pallas import tpu as pltpu
from jax.sharding import PartitionSpec as P

NOPE = 128
ROPE = 64
VDIM = 128
LATENT = 512
WIDE = LATENT + 128
HEADS = 4
MASKED = -1e30
MESH = pl.DeviceIdType.MESH
F32 = jnp.float32
BF16 = jnp.bfloat16


def dot_nt(a, b):
    return lax.dot_general(a, b, (((1,), (1,)), ((), ())), preferred_element_type=F32)


def kernel(
    q_ref, lat_ref, gain_ref, up_ref, wo_ref, pos_ref, out_ref,
    own, kb, qb, wb, ab, acc, high, total, posq, bias,
    o_out, o_in, lse_out, lse_in, stage, parts,
    za_s, za_r, zb_s, zb_r, k1_s, k2_s, k_r, wx_s, wx_r, q_s, q_r,
    w_s, w_r, m_s, m_r, a_s, a_r, p_s, p_r,
):
    c = lax.axis_index("ctx")
    h = lax.axis_index("head")
    xh, z = c // 16, c % 16
    y, xl, core = h // 4, (h // 2) % 2, h % 2
    x = xh * 2 + xl
    chip = h // 2
    other = 1 - core

    def dev(x_, y_, z_, core_):
        return ((x_ // 2) * 16 + z_, y_ * 4 + (x_ % 2) * 2 + core_)

    def remote(src, dst, send, recv, to):
        return pltpu.make_async_remote_copy(
            src_ref=src, dst_ref=dst, send_sem=send, recv_sem=recv, device_id=to, device_id_type=MESH
        )

    barrier = pltpu.get_barrier_semaphore()
    z_offsets = (1, 15, 2, 14, 4, 12, 8)
    for o in z_offsets:
        pl.semaphore_signal(barrier, inc=1, device_id=dev(x, y, (z + o) % 16, core), device_id_type=MESH)
    for dx in range(4):
        for dy in range(4):
            for dk in range(2):
                if dx or dy or dk:
                    to = dev((x + dx) % 4, (y + dy) % 4, z, (core + dk) % 2)
                    pl.semaphore_signal(barrier, inc=1, device_id=to, device_id_type=MESH)

    pos = pos_ref[...]
    posf = pos.astype(F32)
    freq = jnp.exp(
        lax.broadcasted_iota(jnp.int32, (ROPE // 2, 128), 0).astype(F32) * (-2.0 * math.log(10000.0) / ROPE)
    )
    angles = posf * freq
    cosine, sine = jnp.cos(angles), jnp.sin(angles)
    nope = lat_ref[:LATENT, :].astype(F32)
    mean_square = jnp.mean(nope * nope, axis=0, keepdims=True)
    nope = nope * lax.rsqrt(mean_square + 1e-06)
    front = lat_ref[LATENT : LATENT + 32, :].astype(F32)
    back = lat_ref[LATENT + 32 :, :].astype(F32)
    row = lax.broadcasted_iota(jnp.int32, (64, 128), 0)
    places = jnp.where(
        row == 0, jnp.right_shift(pos, 6).astype(F32), jnp.where(row == 1, jnp.bitwise_and(pos, 63).astype(F32), 0.0)
    )
    tail = jnp.concatenate([front * cosine - back * sine, back * cosine + front * sine, places], axis=0)
    own[:, :LATENT] = (nope.T * gain_ref[...]).astype(BF16)
    own[:, LATENT:] = tail.T.astype(BF16)
    posq[...] = jnp.broadcast_to(posf, (128, 128)).T
    wb[z, core] = wo_ref[pl.ds(pl.multiple_of(core * 112, 16), 112), :]

    pl.semaphore_wait(barrier, 38)

    mine = (z % 2) == core
    slice_rows = pl.ds(pl.multiple_of(chip * 16, 16), 16)

    def za_copy(a):
        return remote(
            own.at[slice_rows], kb.at[0, y, x, pl.ds(16 * a, 16)], za_s.at[a - 1], za_r.at[a - 1],
            dev(x, y, (z + 4 * a) % 16, core),
        )

    @pl.when(mine)
    def _():
        for a in (1, 3, 2):
            za_copy(a).start()
        kb[0, y, x, 0:16, :] = own[slice_rows, :]

    wx = remote(
        wo_ref.at[pl.ds(pl.multiple_of(other * 112, 16), 112)], wb.at[z, core], wx_s, wx_r, dev(x, y, z, other)
    )
    wx.start()

    def unit_place(way, u):
        dist = u // 2 + 1
        head = core if u % 2 == 0 and not (u == 14 and way == 1) else other
        held = (z - (dist - 1)) % 16 if way == 0 else (z + (dist - 1)) % 16
        near = (z + 1) % 16 if way == 0 else (z + 15) % 16
        return held, near, head

    def w_copy(way, u):
        held, near, head = unit_place(way, u)
        return remote(
            wb.at[held, head], wb.at[held, head], w_s.at[way, u], w_r.at[way, u], dev(x, y, near, core)
        )

    def w_wait(way, u):
        dist = u // 2 + 1
        block = (z - dist) % 16 if way == 0 else (z + dist) % 16
        head = unit_place(way, u)[2]
        remote(
            wb.at[block, head], wb.at[block, head], w_s.at[way, u], w_r.at[way, u], dev(x, y, z, other)
        ).wait_recv()

    def serve(u):
        for way in (0, 1):
            w_wait(way, u)
            if u < 12:
                w_copy(way, u + 2).start()
            elif (u, way) in ((12, 0), (13, 1)):
                w_copy(way, 14).start()

    for way in (0, 1):
        w_copy(way, 0).start()

    scale = (NOPE + ROPE) ** -0.5 * math.log2(math.e)
    cos_all = jnp.concatenate([cosine] * 4, axis=0).T
    sin_all = jnp.concatenate([-sine, sine, -sine, sine], axis=0).T
    lane = lax.broadcasted_iota(jnp.int32, (128, 128), 1)
    for pair in range(HEADS // 2):
        both = q_ref[:, pair * 384 : (pair + 1) * 384]
        rest = pltpu.roll(both[:, 128:].astype(F32), 192, 1)
        ropes = rest[:, 128:]
        swapped = jnp.where((lane // 32) % 2 == 0, pltpu.roll(ropes, 96, 1), pltpu.roll(ropes, 32, 1))
        turned = (ropes * cos_all + swapped * sin_all) * scale
        for i in range(2):
            n = pair * 2 + i
            plain = both[:, :128] if i == 0 else rest[:, :128].astype(BF16)
            absorbed = dot_nt(plain, up_ref[:, 256 * n : 256 * n + 128]) * scale
            rope = pltpu.roll(turned, 64, 1) if i == 0 else turned
            qb[core * 4 + n, :, :LATENT] = absorbed.astype(BF16)
            qb[core * 4 + n, :, LATENT:] = jnp.where(lane < 64, rope, 0.0).astype(BF16)
    q_copy = remote(
        qb.at[pl.ds(core * 4, 4)], qb.at[pl.ds(core * 4, 4)], q_s, q_r, dev(x, y, z, other)
    )
    q_copy.start()

    wx_in = remote(wb.at[z, other], wb.at[z, other], wx_s, wx_r, dev(x, y, z, other))
    wx_in.wait_recv()
    for way in (0, 1):
        w_copy(way, 1).start()

    def zb_copy(i):
        dst = kb.at[0, y, x] if i == 0 else kb.at[1, x, y]
        to = (z + (1, 15, 2)[i]) % 16
        return remote(kb.at[0, y, x], dst, zb_s.at[i], zb_r.at[min(i, 1)], dev(x, y, to, core))

    def zb_wait(half):
        dst = kb.at[0, y, x] if half == 0 else kb.at[1, x, y]
        remote(dst, dst, zb_s.at[0], zb_r.at[half], dev(x, y, z, other)).wait_recv()

    @pl.when(mine)
    def _():
        for a in (1, 3, 2):
            za_copy(a).wait_recv()
        for i in range(3):
            zb_copy(i).start()

    @pl.when(jnp.logical_not(mine))
    def _():
        zb_wait(0)

    def place(f):
        return (y, x) if f == 0 else (x, y)

    def peer(f, along_a, i):
        moves_y = (f == 0) == along_a
        if moves_y:
            return dev(x, (y + i) % 4, z, core)
        return dev((x + i) % 4, y, z, core)

    def k1_copy(f, along_a, i):
        a, b = place(f)
        return remote(
            kb.at[f, a, b], kb.at[f, a, b], k1_s.at[f, int(along_a) * 3 + i - 1], k_r.at[f, a, b], peer(f, along_a, i)
        )

    def k2_copy(f, j, i):
        a, b = place(f)
        b = (b + j) % 4
        return remote(
            kb.at[f, a, b], kb.at[f, a, b], k2_s.at[f, j - 1, i - 1], k_r.at[f, a, b], peer(f, True, i)
        )

    def k_wait(f, a, b):
        remote(
            kb.at[f, a, b], kb.at[f, a, b], k1_s.at[f, 0], k_r.at[f, a, b], dev(x, y, z, other)
        ).wait_recv()

    for i in (1, 3, 2):
        k1_copy(0, False, i).start()
    for i in (1, 3, 2):
        k1_copy(0, True, i).start()
    zb_wait(1)
    for i in (1, 3, 2):
        k1_copy(1, False, i).start()
    for i in (1, 3, 2):
        k1_copy(1, True, i).start()

    serve(0)
    for j in (1, 3, 2):
        for f in (0, 1):
            a, b = place(f)
            k_wait(f, a, (b + j) % 4)
            for i in (1, 3, 2):
                k2_copy(f, j, i).start()
    serve(1)

    high[...] = jnp.full_like(high, MASKED)
    total[...] = jnp.zeros_like(total)
    acc[...] = jnp.zeros_like(acc)
    remote(
        qb.at[pl.ds(other * 4, 4)], qb.at[pl.ds(other * 4, 4)], q_s, q_r, dev(x, y, z, other)
    ).wait_recv()
    lane8 = lax.broadcasted_iota(jnp.int32, (8, WIDE), 1)
    pick = jnp.where(
        lane8 == LATENT + ROPE, 64.0, jnp.where(lane8 == LATENT + ROPE + 1, 1.0, 0.0)
    ).astype(BF16)

    def attend(f, a):
        keys = kb[f, a].reshape(256, WIDE)
        posk = dot_nt(pick, keys)[0:1, :]
        for i in range(2):
            bias[:, i * 128 : (i + 1) * 128] = jnp.where(posk[:, i * 128 : (i + 1) * 128] <= posq[...], 0.0, MASKED)

        def rows(p, carry):
            queries = qb[pl.ds(p * 2, 2)].reshape(256, WIDE)
            block = kb[f, a].reshape(256, WIDE)
            masks = bias[...]
            scores = dot_nt(queries, block) + jnp.concatenate([masks, masks], axis=0)
            before = high[p]
            raised = jnp.maximum(before, jnp.max(scores, axis=1, keepdims=True))
            terms = jnp.exp2(scores - raised[:, :1])
            rescale = jnp.exp2(before - raised)
            high[p] = raised
            total[p] = total[p] * rescale + terms[:, :128] + terms[:, 128:]
            acc[p] = acc[p] * rescale[:, :1] + jnp.dot(
                terms.astype(BF16), block[:, :LATENT], preferred_element_type=F32
            )
            return carry

        lax.fori_loop(0, 4, rows, 0)

    step = 2
    for i in (0, 1, 3, 2):
        for f in (0, 1):
            a, b = place(f)
            a = (a + i) % 4
            if i:
                for j in range(4):
                    k_wait(f, a, (b + j) % 4)
            attend(f, a)
            serve(step)
            step += 1

    for t in range(2):
        p = other * 2 + t
        sums = jnp.sum(total[p], axis=1, keepdims=True)
        o_out[t] = (acc[p] / sums).astype(BF16)
        lse_out[t] = high[p] + jnp.log2(sums)
    m_copies = [
        remote(o_out, o_in, m_s.at[0], m_r.at[0], dev(x, y, z, other)),
        remote(lse_out, lse_in, m_s.at[1], m_r.at[1], dev(x, y, z, other)),
    ]
    for copy in m_copies:
        copy.start()
    serve(step)
    for copy in m_copies:
        copy.wait_recv()
    for t in range(2):
        p = core * 2 + t
        sums = jnp.sum(total[p], axis=1, keepdims=True)
        lse = high[p] + jnp.log2(sums)
        largest = jnp.maximum(lse, lse_in[t])
        one, two = jnp.exp2(lse - largest), jnp.exp2(lse_in[t] - largest)
        share = two / (one + two)
        merged = acc[p] * ((one / (one + two))[:, :1] / sums) + o_in[t].astype(F32) * share[:, :1]
        merged = merged.astype(BF16)
        for i in range(2):
            n = t * 2 + i
            ab[core, xh, :, n * 128 : (n + 1) * 128] = jnp.dot(
                merged[i * 128 : (i + 1) * 128], up_ref[:, 256 * n + 128 : 256 * n + 256], preferred_element_type=F32
            ).astype(BF16)

    x2 = (x + 2) % 4
    a_copies = [
        remote(ab.at[core, xh], ab.at[core, xh], a_s.at[i], a_r.at[core, xh], to)
        for i, to in enumerate((dev(x2, y, z, core), dev(x2, y, z, other), dev(x, y, z, other)))
    ]
    for copy in a_copies:
        copy.start()
    serve(step + 1)
    for k, r in ((other, xh), (core, 1 - xh), (other, 1 - xh)):
        remote(ab.at[k, r], ab.at[k, r], a_s.at[0], a_r.at[k, r], dev(x, y, z, other)).wait_recv()

    def p_copy(zb, r):
        head = (xh * 16 + zb) // 2
        dst = parts.at[chip, zb % 2, core]
        return (
            jnp.logical_and(head == h, xh == r),
            remote(stage.at[zb, r], dst, p_s.at[zb, r], p_r, (r * 16 + z, head)),
            pltpu.make_async_copy(stage.at[zb, r], dst, p_r),
        )

    def project(zb):
        made = dot_nt(wb[zb, 0], ab[0].reshape(256, 512)) + dot_nt(wb[zb, 1], ab[1].reshape(256, 512))
        made = made.astype(BF16)
        for r in range(2):
            stage[zb, r] = made[:, r * 128 : (r + 1) * 128]
            stays, far, near = p_copy(zb, r)
            pl.when(jnp.logical_not(stays))(far.start)
            pl.when(stays)(near.start)

    def project_both(dist):
        def one(i, carry):
            project((z + jnp.where(i == 0, dist, 16 - dist)) % 16)
            return carry

        lax.fori_loop(0, 2, one, 0)

    project(z)
    for dist in range(1, 5):
        project_both(dist)
    serve(12)
    project_both(5)
    project_both(6)
    serve(13)
    project_both(7)
    serve(14)
    project((z + 8) % 16)

    remote(parts, parts, p_s.at[0, 0], p_r, dev(x, y, z, other)).wait_recv()
    result = parts[0].reshape(448, 128).astype(F32)
    for i in range(1, 8):
        result = result + parts[i].reshape(448, 128).astype(F32)
    out_ref[...] = result.astype(BF16)

    @pl.when(mine)
    def _():
        for a in (1, 3, 2):
            za_copy(a).wait_send()
        for i in range(3):
            zb_copy(i).wait_send()

    for f in (0, 1):
        for i in (1, 2, 3):
            k1_copy(f, False, i).wait_send()
            k1_copy(f, True, i).wait_send()
            for j in (1, 2, 3):
                k2_copy(f, j, i).wait_send()
    wx.wait_send()
    q_copy.wait_send()
    for way in (0, 1):
        for u in range(15):
            w_copy(way, u).wait_send()
    for copy in m_copies + a_copies:
        copy.wait_send()

    def p_done(zb, carry):
        for r in range(2):
            stays, far, _ = p_copy(zb, r)
            pl.when(jnp.logical_not(stays))(far.wait_send)
        return carry

    lax.fori_loop(0, 16, p_done, 0)


def shards(queries, latents, latent_gain, latent_up, out_weight, positions):
    dma = pltpu.SemaphoreType.DMA
    vmem = pltpu.VMEM
    made = pl.pallas_call(
        kernel,
        out_shape=jax.ShapeDtypeStruct((448, 128), BF16),
        in_specs=[pl.BlockSpec(memory_space=pltpu.VMEM)] * 6,
        out_specs=pl.BlockSpec(memory_space=pltpu.VMEM),
        scratch_shapes=[
            vmem((128, WIDE), BF16),
            vmem((2, 4, 4, 64, WIDE), BF16),
            vmem((8, 128, WIDE), BF16),
            vmem((16, 2, 112, 512), BF16),
            vmem((2, 2, 128, 512), BF16),
            vmem((4, 256, 512), F32),
            vmem((4, 256, 128), F32),
            vmem((4, 256, 128), F32),
            vmem((128, 128), F32),
            vmem((128, 256), F32),
            vmem((2, 256, 512), BF16),
            vmem((2, 256, 512), BF16),
            vmem((2, 256, 128), F32),
            vmem((2, 256, 128), F32),
            vmem((16, 2, 112, 128), BF16),
            vmem((8, 2, 2, 112, 128), BF16),
            dma((3,)), dma((3,)), dma((3,)), dma((2,)),
            dma((2, 6)), dma((2, 3, 3)), dma((2, 4, 4)),
            dma, dma, dma, dma,
            dma((2, 15)), dma((2, 15)), dma((2,)), dma((2,)),
            dma((3,)), dma((2, 2)), dma((16, 2)), dma,
        ],
        compiler_params=pltpu.CompilerParams(
            collective_id=0, has_side_effects=True, vmem_limit_bytes=48 * 1024 * 1024
        ),
        cost_estimate=pl.CostEstimate(flops=8_000_000_000, bytes_accessed=4_000_000, transcendentals=2_200_000),
    )(
        queries, latents.T, latent_gain.reshape(1, 512), latent_up, out_weight.T, positions.reshape(1, 128)
    )
    return made.T


def solution(mesh):
    in_specs = (P("ctx", "head"), P("ctx", None), P(), P(None, "head"), P("head", "ctx"), P("ctx"))
    out_specs = P("ctx", "head")
    return jax.shard_map(shards, mesh=mesh, in_specs=in_specs, out_specs=out_specs, check_vma=False)
```

```python
import functools
import math

import jax
import jax.numpy as jnp
from jax import lax
from jax.experimental import pallas as pl
from jax.experimental.pallas import tpu as pltpu
from jax.sharding import PartitionSpec as P

NOPE = 128
ROPE = 64
VDIM = 128
LATENT = 512
WIDE = LATENT + 128
HEADS = 4
MASKED = -1e30
MESH = pl.DeviceIdType.MESH
F32 = jnp.float32
BF16 = jnp.bfloat16


def dot_nt(a, b):
    return lax.dot_general(a, b, (((1,), (1,)), ((), ())), preferred_element_type=F32)


def kernel(
    q_hbm, lat_hbm, gain_hbm, up_hbm, wo_hbm, pos_hbm, out_ref,
    q_ref, lat_ref, gain_ref, up_ref, pos_ref,
    own, kb, qb, wb, ab, scores, posq, bias,
    o_out, o_in, lse_out, lse_in, stage, parts,
    z_s, z_r, k1_s, k2_s, k3_s, k_r, wx_s, wx_r, q_s, q_r,
    w_s, w_r, m_s, m_r, a_s, a_r, p_s, p_r, in_s,
):
    c = lax.axis_index("ctx")
    h = lax.axis_index("head")
    xh, z = c // 16, c % 16
    y, xl, core = h // 4, (h // 2) % 2, h % 2
    x = xh * 2 + xl
    chip = h // 2
    other = 1 - core

    def dev(x_, y_, z_, core_):
        return ((x_ // 2) * 16 + z_, y_ * 4 + (x_ % 2) * 2 + core_)

    def remote(src, dst, send, recv, to):
        return pltpu.make_async_remote_copy(
            src_ref=src, dst_ref=dst, send_sem=send, recv_sem=recv, device_id=to, device_id_type=MESH
        )

    loads = [
        pltpu.make_async_copy(src, dst, in_s.at[i])
        for i, (src, dst) in enumerate((
            (pos_hbm, pos_ref), (lat_hbm, lat_ref), (gain_hbm, gain_ref), (q_hbm, q_ref), (up_hbm, up_ref),
            (wo_hbm.at[pl.ds(pl.multiple_of(core * 112, 16), 112)], wb.at[core, 0]),
        ))
    ]
    for load in loads:
        load.start()

    barrier = pltpu.get_barrier_semaphore()
    for o in range(1, 16):
        pl.semaphore_signal(barrier, inc=1, device_id=dev(x, y, (z + o) % 16, core), device_id_type=MESH)
    for dx in range(4):
        for dy in range(4):
            for dk in range(2):
                if dx or dy or dk:
                    to = dev((x + dx) % 4, (y + dy) % 4, z, (core + dk) % 2)
                    pl.semaphore_signal(barrier, inc=1, device_id=to, device_id_type=MESH)


    wx = remote(
        wo_hbm.at[pl.ds(pl.multiple_of(other * 112, 16), 112)], wb.at[core, 0], wx_s, wx_r, dev(x, y, z, other)
    )
    pl.semaphore_wait(barrier, 46)
    wx.start()

    def slot_of(way, dist):
        return 0 if dist == 0 else 15 if dist == 8 else 2 * dist - 1 + way

    def w_copy(way, u):
        dist = u // 2 + 1
        head = core if u % 2 == 0 and not (u == 14 and way == 1) else other
        near = (z + 1) % 16 if way == 0 else (z + 15) % 16
        return remote(
            wb.at[head, slot_of(way, dist - 1)], wb.at[head, slot_of(way, dist)],
            w_s.at[way, u], w_r.at[way, u], dev(x, y, near, core),
        )

    def w_wait(way, u):
        w_copy(way, u).wait_recv()

    def serve(u):
        for way in (0, 1):
            w_wait(way, u)
            if u < 12:
                w_copy(way, u + 2).start()
            elif (u, way) in ((12, 0), (13, 1)):
                w_copy(way, 14).start()

    loads[5].wait()
    for way in (0, 1):
        w_copy(way, 0).start()

    for load in loads[:3]:
        load.wait()

    pos = pos_ref[...]
    posf = pos.astype(F32)
    freq = jnp.exp(
        lax.broadcasted_iota(jnp.int32, (ROPE // 2, 128), 0).astype(F32) * (-2.0 * math.log(10000.0) / ROPE)
    )
    angles = posf * freq
    cosine, sine = jnp.cos(angles), jnp.sin(angles)
    nope = lat_ref[:LATENT, :].astype(F32)
    mean_square = jnp.mean(nope * nope, axis=0, keepdims=True)
    nope = nope * lax.rsqrt(mean_square + 1e-06)
    front = lat_ref[LATENT : LATENT + 32, :].astype(F32)
    back = lat_ref[LATENT + 32 :, :].astype(F32)
    row = lax.broadcasted_iota(jnp.int32, (64, 128), 0)
    places = jnp.where(
        row == 0, jnp.right_shift(pos, 6).astype(F32), jnp.where(row == 1, jnp.bitwise_and(pos, 63).astype(F32), 0.0)
    )
    tail = jnp.concatenate([front * cosine - back * sine, back * cosine + front * sine, places], axis=0)
    own[:, :LATENT] = (nope.T * gain_ref[...]).astype(BF16)
    own[:, LATENT:] = tail.T.astype(BF16)
    posq[...] = jnp.broadcast_to(posf, (128, 128)).T

    mine = (z % 2) == core
    slice_rows = pl.ds(pl.multiple_of(chip * 16, 16), 16)
    from_even = (0, -2, 2, -4, 4, -6, 6, 8)
    from_odd = (-1, 1, -3, 3, -5, 5, -7, 7)

    def place(f):
        return (y, x) if f == 0 else (x, y)

    def slice_at(n):
        f, t = (n // 2) % 2, n // 4
        return kb.at[(f, *place(f), pl.ds(32 * t + 16 * (n % 2), 16))]

    def z_copy(o):
        n = from_odd.index(-o) if o % 2 else from_even.index(8 if o == 8 else -o)
        return remote(
            own.at[slice_rows], slice_at(n), z_s.at[o % 16 - 1], z_r.at[n], dev(x, y, (z + o) % 16, core)
        )

    def z_wait(n):
        remote(slice_at(n), slice_at(n), z_s.at[0], z_r.at[n], dev(x, y, z, other)).wait_recv()

    z_order = (1, -1, 2, -2, 3, -3, 4, -4, 5, -5, 6, -6, 7, -7, 8)

    @pl.when(mine)
    def _():
        for o in z_order:
            z_copy(o).start()
        kb[0, y, x, 0:16, :] = own[slice_rows, :]

    wx_in = remote(wb.at[other, 0], wb.at[other, 0], wx_s, wx_r, dev(x, y, z, other))
    wx_in.wait_recv()
    for way in (0, 1):
        w_copy(way, 1).start()

    for load in loads[3:5]:
        load.wait()
    scale = (NOPE + ROPE) ** -0.5 * math.log2(math.e)
    cos_all = jnp.concatenate([cosine] * 4, axis=0).T
    sin_all = jnp.concatenate([-sine, sine, -sine, sine], axis=0).T
    lane = lax.broadcasted_iota(jnp.int32, (128, 128), 1)
    for pair in range(HEADS // 2):
        both = q_ref[:, pair * 384 : (pair + 1) * 384]
        rest = pltpu.roll(both[:, 128:].astype(F32), 192, 1)
        ropes = rest[:, 128:]
        swapped = jnp.where((lane // 32) % 2 == 0, pltpu.roll(ropes, 96, 1), pltpu.roll(ropes, 32, 1))
        turned = (ropes * cos_all + swapped * sin_all) * scale
        for i in range(2):
            n = pair * 2 + i
            plain = both[:, :128] if i == 0 else rest[:, :128].astype(BF16)
            absorbed = dot_nt(plain, up_ref[:, 256 * n : 256 * n + 128]) * scale
            rope = pltpu.roll(turned, 64, 1) if i == 0 else turned
            qb[core * 4 + n, :, :LATENT] = absorbed.astype(BF16)
            qb[core * 4 + n, :, LATENT:] = jnp.where(lane < 64, rope, 0.0).astype(BF16)
    q_copy = remote(
        qb.at[pl.ds(core * 4, 4)], qb.at[pl.ds(core * 4, 4)], q_s, q_r, dev(x, y, z, other)
    )
    q_copy.start()

    def peer(f, along_a, i):
        moves_y = (f == 0) == along_a
        if moves_y:
            return dev(x, (y + i) % 4, z, core)
        return dev((x + i) % 4, y, z, core)

    def piece(f, a, b, t):
        return kb.at[f, a, b, pl.ds(32 * t, 32)], k_r.at[f, a, b, t]

    def k1_copy(f, t, i):
        a, b = place(f)
        ref, got = piece(f, a, b, t)
        return remote(ref, ref, k1_s.at[f, t, i - 1], got, peer(f, False, i))

    def k2_copy(f, t, j, side):
        a, b = place(f)
        ref, got = piece(f, a, (b + j) % 4, t)
        return remote(ref, ref, k2_s.at[f, t, j, side], got, peer(f, True, 1 if side == 0 else 3))

    def k3_copy(f, t, j):
        a, b = place(f)
        ref, got = piece(f, (a + (3, 1)[t]) % 4, (b + j) % 4, t)
        return remote(ref, ref, k3_s.at[f, t, j], got, peer(f, True, (1, 3)[t]))

    def k_wait(f, t, i, j):
        a, b = place(f)
        ref, got = piece(f, (a + i) % 4, (b + j) % 4, t)
        remote(ref, ref, k3_s.at[f, t, 0], got, dev(x, y, z, other)).wait_recv()

    for part in range(4):
        f, t = part % 2, part // 2
        if part == 0:
            pl.when(jnp.logical_not(mine))(functools.partial(z_wait, 0))
        else:
            z_wait(2 * part)
        z_wait(2 * part + 1)
        for i in (1, 3, 2):
            k1_copy(f, t, i).start()
        for side in (0, 1):
            k2_copy(f, t, 0, side).start()
        serve(part)

    def spread(t):
        for j in (1, 3, 2):
            for f in (0, 1):
                k_wait(f, t, 0, j)
                for side in (0, 1):
                    k2_copy(f, t, j, side).start()

    def relay(t):
        for j in (0, 1, 3, 2):
            for f in (0, 1):
                k_wait(f, t, (3, 1)[t], j)
                k3_copy(f, t, j).start()

    spread(0)
    serve(4)
    spread(1)
    serve(5)
    relay(0)
    serve(6)

    remote(
        qb.at[pl.ds(other * 4, 4)], qb.at[pl.ds(other * 4, 4)], q_s, q_r, dev(x, y, z, other)
    ).wait_recv()
    lane8 = lax.broadcasted_iota(jnp.int32, (8, WIDE), 1)
    pick = jnp.where(
        lane8 == LATENT + ROPE, 64.0, jnp.where(lane8 == LATENT + ROPE + 1, 1.0, 0.0)
    ).astype(BF16)

    def score(f, a):
        posk = dot_nt(pick, kb[f, a].reshape(256, WIDE))[0:1, :]
        for i in range(2):
            bias[:, i * 128 : (i + 1) * 128] = jnp.where(posk[:, i * 128 : (i + 1) * 128] <= posq[...], 0.0, MASKED)
        for p in range(4):
            masks = bias[...]
            scores[f * 4 + a, p] = dot_nt(
                qb[2 * p : 2 * p + 2].reshape(256, WIDE), kb[f, a].reshape(256, WIDE)
            ) + jnp.concatenate([masks, masks], axis=0)

    step = 7
    for i in (0, 1, 3, 2):
        for f in (0, 1):
            if i:
                for t in (0, 1):
                    if (i, t) not in ((3, 0), (1, 1)):
                        for j in range(4):
                            k_wait(f, t, i, j)
            score(f, (place(f)[0] + i) % 4)
            if (i, f) == (0, 0):
                relay(1)
            elif f == 1:
                serve(step)
                step += 1

    def soften(p):
        parts_of = [scores[u, p] for u in range(8)]
        largest = parts_of[0]
        for one in parts_of[1:]:
            largest = jnp.maximum(largest, one)
        largest = jnp.max(largest, axis=1, keepdims=True)
        terms = [jnp.exp2(one - largest) for one in parts_of]
        sums = terms[0]
        for one in terms[1:]:
            sums = sums + one
        sums = jnp.sum(sums, axis=1, keepdims=True)
        mixed = jnp.dot(
            jnp.concatenate([one.astype(BF16) for one in terms], axis=1),
            kb[:, :, :, :, :LATENT].reshape(2048, LATENT),
            preferred_element_type=F32,
        )
        return mixed / sums, jnp.broadcast_to(largest + jnp.log2(sums), (256, 128))

    def m_copy(t, i):
        src, dst = ((o_out, o_in), (lse_out, lse_in))[i]
        return remote(src.at[t], dst.at[t], m_s.at[t, i], m_r.at[t, i], dev(x, y, z, other))

    def a_copy(t, i):
        r = xh if i < 2 else 1 - xh
        to = dev((x + 2) % 4, y, z, core) if i == 0 else dev(x, y, z, other)
        return remote(ab.at[core, t, r], ab.at[core, t, r], a_s.at[t, i], a_r.at[t, core, r], to)

    def a_wait(t, k, r):
        remote(ab.at[k, t, r], ab.at[k, t, r], a_s.at[t, 0], a_r.at[t, k, r], dev(x, y, z, other)).wait_recv()

    for t in range(2):
        mixed, lse_out[t] = soften(other * 2 + t)
        o_out[t] = mixed.astype(BF16)
        for i in range(2):
            m_copy(t, i).start()
    serve(step)
    for t in range(2):
        mixed, lse = soften(core * 2 + t)
        for i in range(2):
            m_copy(t, i).wait_recv()
        largest = jnp.maximum(lse, lse_in[t])
        one, two = jnp.exp2(lse - largest), jnp.exp2(lse_in[t] - largest)
        share = two / (one + two)
        merged = mixed * (one / (one + two))[:, :1] + o_in[t].astype(F32) * share[:, :1]
        merged = merged.astype(BF16)
        for i in range(2):
            n = t * 2 + i
            ab[core, t, xh, :, i * 128 : (i + 1) * 128] = jnp.dot(
                merged[i * 128 : (i + 1) * 128], up_ref[:, 256 * n + 128 : 256 * n + 256], preferred_element_type=F32
            ).astype(BF16)
        a_copy(t, 0).start()
        a_copy(t, 1).start()
    for t in range(2):
        a_wait(t, core, 1 - xh)
        a_copy(t, 2).start()
    for t in range(2):
        a_wait(t, other, xh)
        a_wait(t, other, 1 - xh)

    def p_copy(slot, r):
        dist = (slot + 1) // 2
        zb = (z - dist) % 16 if slot % 2 else (z + dist) % 16
        head = (xh * 16 + zb) // 2
        dst = parts.at[chip, zb % 2, core]
        return (
            jnp.logical_and(head == h, xh == r),
            remote(stage.at[slot, r], dst, p_s.at[slot, r], p_r, (r * 16 + z, head)),
            pltpu.make_async_copy(stage.at[slot, r], dst, p_r),
        )

    def project(first, count):
        made = None
        for e in range(2):
            for t in range(2):
                weights = wb[e, first : first + count, :, t * 256 : (t + 1) * 256].reshape(count * 112, 256)
                term = dot_nt(weights, ab[e, t].reshape(256, 256))
                made = term if made is None else made + term
        made = made.astype(BF16)
        for i in range(count):
            for r in range(2):
                stage[first + i, r] = made[i * 112 : (i + 1) * 112, r * 128 : (r + 1) * 128]
                stays, far, near = p_copy(first + i, r)
                pl.when(jnp.logical_not(stays))(far.start)
                pl.when(stays)(near.start)

    project(0, 4)
    project(4, 5)
    serve(12)
    project(9, 4)
    serve(13)
    project(13, 2)
    serve(14)
    project(15, 1)

    remote(parts, parts, p_s.at[0, 0], p_r, dev(x, y, z, other)).wait_recv()
    result = parts[0].reshape(448, 128).astype(F32)
    for i in range(1, 8):
        result = result + parts[i].reshape(448, 128).astype(F32)
    out_ref[...] = result.astype(BF16)

    @pl.when(mine)
    def _():
        for o in z_order:
            z_copy(o).wait_send()

    for f in (0, 1):
        for t in (0, 1):
            for i in (1, 2, 3):
                k1_copy(f, t, i).wait_send()
            for j in range(4):
                k3_copy(f, t, j).wait_send()
                for side in (0, 1):
                    k2_copy(f, t, j, side).wait_send()
    wx.wait_send()
    q_copy.wait_send()
    for way in (0, 1):
        for u in range(15):
            w_copy(way, u).wait_send()
    for t in range(2):
        for i in range(2):
            m_copy(t, i).wait_send()
        for i in range(3):
            a_copy(t, i).wait_send()

    for slot in range(16):
        for r in range(2):
            stays, far, _ = p_copy(slot, r)
            pl.when(jnp.logical_not(stays))(far.wait_send)


def shards(queries, latents, latent_gain, latent_up, out_weight, positions):
    dma = pltpu.SemaphoreType.DMA
    vmem = pltpu.VMEM
    made = pl.pallas_call(
        kernel,
        out_shape=jax.ShapeDtypeStruct((448, 128), BF16),
        in_specs=[pl.BlockSpec(memory_space=pltpu.HBM)] * 6,
        out_specs=pl.BlockSpec(memory_space=pltpu.VMEM),
        scratch_shapes=[
            vmem((128, 768), BF16),
            vmem((576, 128), BF16),
            vmem((1, 512), F32),
            vmem((512, 1024), BF16),
            vmem((1, 128), jnp.int32),
            vmem((128, WIDE), BF16),
            vmem((2, 4, 4, 64, WIDE), BF16),
            vmem((8, 128, WIDE), BF16),
            vmem((2, 16, 112, 512), BF16),
            vmem((2, 2, 2, 128, 256), BF16),
            vmem((8, 4, 256, 256), F32),
            vmem((128, 128), F32),
            vmem((128, 256), F32),
            vmem((2, 256, 512), BF16),
            vmem((2, 256, 512), BF16),
            vmem((2, 256, 128), F32),
            vmem((2, 256, 128), F32),
            vmem((16, 2, 112, 128), BF16),
            vmem((8, 2, 2, 112, 128), BF16),
            dma((15,)), dma((8,)),
            dma((2, 2, 3)), dma((2, 2, 4, 2)), dma((2, 2, 4)), dma((2, 4, 4, 2)),
            dma, dma, dma, dma,
            dma((2, 15)), dma((2, 15)), dma((2, 2)), dma((2, 2)),
            dma((2, 3)), dma((2, 2, 2)), dma((16, 2)), dma, dma((6,)),
        ],
        compiler_params=pltpu.CompilerParams(
            collective_id=0, has_side_effects=True, vmem_limit_bytes=62 * 1024 * 1024
        ),
        cost_estimate=pl.CostEstimate(flops=8_000_000_000, bytes_accessed=4_000_000, transcendentals=2_200_000),
    )(
        queries, latents.T, latent_gain.reshape(1, 512), latent_up, out_weight.T, positions.reshape(1, 128)
    )
    return made.T


def solution(mesh):
    in_specs = (P("ctx", "head"), P("ctx", None), P(), P(None, "head"), P("head", "ctx"), P("ctx"))
    out_specs = P("ctx", "head")
    return jax.shard_map(shards, mesh=mesh, in_specs=in_specs, out_specs=out_specs, check_vma=False)
```

```python
import functools
import math

import jax
import jax.numpy as jnp
from jax import lax
from jax.experimental import pallas as pl
from jax.experimental.pallas import tpu as pltpu
from jax.sharding import PartitionSpec as P

NOPE = 128
ROPE = 64
VDIM = 128
LATENT = 512
WIDE = LATENT + 128
HEADS = 4
MASKED = -1e30
MESH = pl.DeviceIdType.MESH
F32 = jnp.float32
BF16 = jnp.bfloat16


def dot_nt(a, b):
    return lax.dot_general(a, b, (((1,), (1,)), ((), ())), preferred_element_type=F32)


def kernel(
    q_hbm, lat_hbm, gain_hbm, up_hbm, wo_hbm, pos_hbm, out_ref,
    q_ref, lat_ref, gain_ref, up_ref, pos_ref,
    own, kb, qb, wb, ab, scores, posq, bias,
    o_out, o_in, lse_out, lse_in, stage, across, halves, parts,
    za_s, za_r, zb_s, zb_r, k1_s, k2_s, k3_s, k_r, wx_s, wx_r, q_s, q_r,
    w_s, w_r, m_s, m_r, a_s, a_r, p_s, p_r, s_s, s_r, in_s,
):
    c = lax.axis_index("ctx")
    h = lax.axis_index("head")
    xh, z = c // 16, c % 16
    y, xl, core = h // 4, (h // 2) % 2, h % 2
    x = xh * 2 + xl
    chip = h // 2
    other = 1 - core

    def dev(x_, y_, z_, core_):
        return ((x_ // 2) * 16 + z_, y_ * 4 + (x_ % 2) * 2 + core_)

    def remote(src, dst, send, recv, to):
        return pltpu.make_async_remote_copy(
            src_ref=src, dst_ref=dst, send_sem=send, recv_sem=recv, device_id=to, device_id_type=MESH
        )

    def wo_part(k, t):
        return wo_hbm.at[pl.ds(pl.multiple_of(k * 112, 16), 112), pl.ds(256 * t, 256)]

    loads = [
        pltpu.make_async_copy(src, dst, in_s.at[i])
        for i, (src, dst) in enumerate((
            (pos_hbm, pos_ref), (lat_hbm, lat_ref), (gain_hbm, gain_ref), (q_hbm, q_ref), (up_hbm, up_ref),
            (wo_part(core, 0), wb.at[core, 0, 0]), (wo_part(core, 1), wb.at[core, 1, 0]),
        ))
    ]
    for load in loads:
        load.start()

    barrier = pltpu.get_barrier_semaphore()
    for o in (1, 15, 2, 14, 4, 12, 8):
        pl.semaphore_signal(barrier, inc=1, device_id=dev(x, y, (z + o) % 16, core), device_id_type=MESH)
    for dx in range(4):
        for dy in range(4):
            for dk in range(2):
                if dx or dy or dk:
                    to = dev((x + dx) % 4, (y + dy) % 4, z, (core + dk) % 2)
                    pl.semaphore_signal(barrier, inc=1, device_id=to, device_id_type=MESH)


    wx = [
        remote(wo_part(other, t), wb.at[core, t, 0], wx_s.at[t], wx_r.at[t], dev(x, y, z, other)) for t in range(2)
    ]
    pl.semaphore_wait(barrier, 38)
    for copy in wx:
        copy.start()

    def slot_of(way, dist):
        return 0 if dist == 0 else 15 if dist == 8 else 2 * dist - 1 + way

    def w_copy(way, u):
        dist, t = u // 4 + 1, u % 2
        head = core if (u % 4 < 2) != (dist == 8 and way == 1) else other
        near = (z + 1) % 16 if way == 0 else (z + 15) % 16
        return remote(
            wb.at[head, t, slot_of(way, dist - 1)], wb.at[head, t, slot_of(way, dist)],
            w_s.at[way, u], w_r.at[way, u], dev(x, y, near, core),
        )

    def serve(k):
        for u in (2 * k, 2 * k + 1):
            for way in (0, 1):
                w_copy(way, u).wait_recv()
                if u < 24:
                    w_copy(way, u + 4).start()
                elif u < 28 and (u - 24) // 2 == way:
                    w_copy(way, 28 + u % 2).start()

    for u in (0, 1):
        loads[5 + u].wait()
        for way in (0, 1):
            w_copy(way, u).start()

    for load in loads[:3]:
        load.wait()

    pos = pos_ref[...]
    posf = pos.astype(F32)
    freq = jnp.exp(
        lax.broadcasted_iota(jnp.int32, (ROPE // 2, 128), 0).astype(F32) * (-2.0 * math.log(10000.0) / ROPE)
    )
    angles = posf * freq
    cosine, sine = jnp.cos(angles), jnp.sin(angles)
    nope = lat_ref[:LATENT, :].astype(F32)
    mean_square = jnp.mean(nope * nope, axis=0, keepdims=True)
    nope = nope * lax.rsqrt(mean_square + 1e-06)
    front = lat_ref[LATENT : LATENT + 32, :].astype(F32)
    back = lat_ref[LATENT + 32 :, :].astype(F32)
    row = lax.broadcasted_iota(jnp.int32, (64, 128), 0)
    places = jnp.where(
        row == 0, jnp.right_shift(pos, 6).astype(F32), jnp.where(row == 1, jnp.bitwise_and(pos, 63).astype(F32), 0.0)
    )
    tail = jnp.concatenate([front * cosine - back * sine, back * cosine + front * sine, places], axis=0)
    own[:, :LATENT] = (nope.T * gain_ref[...]).astype(BF16)
    own[:, LATENT:] = tail.T.astype(BF16)
    posq[...] = jnp.broadcast_to(posf, (128, 128)).T

    mine = (z % 2) == core
    slice_rows = pl.ds(pl.multiple_of(chip * 16, 16), 16)

    def place(f):
        return (y, x) if f == 0 else (x, y)

    def za_copy(i):
        return remote(
            own.at[slice_rows], kb.at[0, y, x, pl.ds(16 * i, 16)], za_s.at[i - 1], za_r.at[i - 1],
            dev(x, y, (z + 4 * i) % 16, core),
        )

    def zb_copy(i, t):
        f = min(i, 1)
        return remote(
            kb.at[0, y, x, pl.ds(32 * t, 32)], kb.at[(f, *place(f), pl.ds(32 * t, 32))],
            zb_s.at[i, t], zb_r.at[f, t], dev(x, y, (z + (1, 15, 2)[i]) % 16, core),
        )

    @pl.when(mine)
    def _():
        for i in (1, 3, 2):
            za_copy(i).start()
        kb[0, y, x, 0:16, :] = own[slice_rows, :]

    for u in (2, 3):
        t = u % 2
        mine_now = wb.at[other, t, 0]
        remote(mine_now, mine_now, wx_s.at[t], wx_r.at[t], dev(x, y, z, other)).wait_recv()
        for way in (0, 1):
            w_copy(way, u).start()

    for load in loads[3:5]:
        load.wait()
    scale = (NOPE + ROPE) ** -0.5 * math.log2(math.e)
    cos_all = jnp.concatenate([cosine] * 4, axis=0).T
    sin_all = jnp.concatenate([-sine, sine, -sine, sine], axis=0).T
    lane = lax.broadcasted_iota(jnp.int32, (128, 128), 1)
    for pair in range(HEADS // 2):
        both = q_ref[:, pair * 384 : (pair + 1) * 384]
        rest = pltpu.roll(both[:, 128:].astype(F32), 192, 1)
        ropes = rest[:, 128:]
        swapped = jnp.where((lane // 32) % 2 == 0, pltpu.roll(ropes, 96, 1), pltpu.roll(ropes, 32, 1))
        turned = (ropes * cos_all + swapped * sin_all) * scale
        for i in range(2):
            n = pair * 2 + i
            plain = both[:, :128] if i == 0 else rest[:, :128].astype(BF16)
            absorbed = dot_nt(plain, up_ref[:, 256 * n : 256 * n + 128]) * scale
            rope = pltpu.roll(turned, 64, 1) if i == 0 else turned
            qb[core * 4 + n, :, :LATENT] = absorbed.astype(BF16)
            qb[core * 4 + n, :, LATENT:] = jnp.where(lane < 64, rope, 0.0).astype(BF16)
    q_copy = remote(
        qb.at[pl.ds(core * 4, 4)], qb.at[pl.ds(core * 4, 4)], q_s, q_r, dev(x, y, z, other)
    )
    q_copy.start()

    def peer(f, along_a, i):
        moves_y = (f == 0) == along_a
        if moves_y:
            return dev(x, (y + i) % 4, z, core)
        return dev((x + i) % 4, y, z, core)

    def piece(f, a, b, t):
        return kb.at[f, a, b, pl.ds(32 * t, 32)], k_r.at[f, a, b, t]

    def k1_copy(f, t, i):
        a, b = place(f)
        ref, got = piece(f, a, b, t)
        return remote(ref, ref, k1_s.at[f, t, i - 1], got, peer(f, False, i))

    def k2_copy(f, t, j, side):
        a, b = place(f)
        ref, got = piece(f, a, (b + j) % 4, t)
        return remote(ref, ref, k2_s.at[f, t, j, side], got, peer(f, True, 1 if side == 0 else 3))

    def k3_copy(f, t, j):
        a, b = place(f)
        ref, got = piece(f, (a + (3, 1)[t]) % 4, (b + j) % 4, t)
        return remote(ref, ref, k3_s.at[f, t, j], got, peer(f, True, (1, 3)[t]))

    def k_wait(f, t, i, j):
        a, b = place(f)
        ref, got = piece(f, (a + i) % 4, (b + j) % 4, t)
        remote(ref, ref, k3_s.at[f, t, 0], got, dev(x, y, z, other)).wait_recv()

    serve(0)
    for f, t in ((0, 0), (0, 1), (1, 0), (1, 1)):
        if f == 0:

            @pl.when(mine)
            def _():
                for i in ((1,), (2, 3))[t]:
                    za_copy(i).wait_recv()
                for i in range(3):
                    zb_copy(i, t).start()

            pl.when(jnp.logical_not(mine))(zb_copy(0, t).wait_recv)
        else:
            zb_copy(1, t).wait_recv()
        for i in (1, 3, 2):
            k1_copy(f, t, i).start()
        for side in (0, 1):
            k2_copy(f, t, 0, side).start()
        if t == 1:
            serve(f + 1)

    def spread(t):
        for j in (1, 3, 2):
            for f in (0, 1):
                k_wait(f, t, 0, j)
                for side in (0, 1):
                    k2_copy(f, t, j, side).start()

    def relay(t):
        for j in (0, 1, 3, 2):
            for f in (0, 1):
                k_wait(f, t, (3, 1)[t], j)
                k3_copy(f, t, j).start()

    spread(0)
    serve(3)
    spread(1)
    serve(4)
    relay(0)
    serve(5)

    remote(
        qb.at[pl.ds(other * 4, 4)], qb.at[pl.ds(other * 4, 4)], q_s, q_r, dev(x, y, z, other)
    ).wait_recv()
    lane8 = lax.broadcasted_iota(jnp.int32, (8, WIDE), 1)
    pick = jnp.where(
        lane8 == LATENT + ROPE, 64.0, jnp.where(lane8 == LATENT + ROPE + 1, 1.0, 0.0)
    ).astype(BF16)

    def score(f, a):
        posk = dot_nt(pick, kb[f, a].reshape(256, WIDE))[0:1, :]
        for i in range(2):
            bias[:, i * 128 : (i + 1) * 128] = jnp.where(posk[:, i * 128 : (i + 1) * 128] <= posq[...], 0.0, MASKED)
        for p in range(4):
            masks = bias[...]
            scores[f * 4 + a, p] = dot_nt(
                qb[2 * p : 2 * p + 2].reshape(256, WIDE), kb[f, a].reshape(256, WIDE)
            ) + jnp.concatenate([masks, masks], axis=0)

    step = 6
    for i in (0, 1, 3, 2):
        for f in (0, 1):
            if i:
                for t in (0, 1):
                    if (i, t) not in ((3, 0), (1, 1)):
                        for j in range(4):
                            k_wait(f, t, i, j)
            score(f, (place(f)[0] + i) % 4)
            if (i, f) == (0, 0):
                relay(1)
            elif f == 1:
                serve(step)
                step += 1

    def soften(p):
        parts_of = [scores[u, p] for u in range(8)]
        largest = parts_of[0]
        for one in parts_of[1:]:
            largest = jnp.maximum(largest, one)
        largest = jnp.max(largest, axis=1, keepdims=True)
        terms = [jnp.exp2(one - largest) for one in parts_of]
        sums = terms[0]
        for one in terms[1:]:
            sums = sums + one
        sums = jnp.sum(sums, axis=1, keepdims=True)
        mixed = jnp.dot(
            jnp.concatenate([one.astype(BF16) for one in terms], axis=1),
            kb[:, :, :, :, :LATENT].reshape(2048, LATENT),
            preferred_element_type=F32,
        )
        return mixed / sums, jnp.broadcast_to(largest + jnp.log2(sums), (256, 128))

    def m_copy(t, i):
        src, dst = ((o_out, o_in), (lse_out, lse_in))[i]
        return remote(src.at[t], dst.at[t], m_s.at[t, i], m_r.at[t, i], dev(x, y, z, other))

    def a_copy(t, i):
        r = xh if i < 2 else 1 - xh
        to = dev((x + 2) % 4, y, z, core) if i == 0 else dev(x, y, z, other)
        return remote(ab.at[core, t, r], ab.at[core, t, r], a_s.at[t, i], a_r.at[t, core, r], to)

    def a_wait(t, k, r):
        remote(ab.at[k, t, r], ab.at[k, t, r], a_s.at[t, 0], a_r.at[t, k, r], dev(x, y, z, other)).wait_recv()

    for t in range(2):
        mixed, lse_out[t] = soften(other * 2 + t)
        o_out[t] = mixed.astype(BF16)
        for i in range(2):
            m_copy(t, i).start()
    serve(10)
    for t in range(2):
        mixed, lse = soften(core * 2 + t)
        for i in range(2):
            m_copy(t, i).wait_recv()
        largest = jnp.maximum(lse, lse_in[t])
        one, two = jnp.exp2(lse - largest), jnp.exp2(lse_in[t] - largest)
        share = two / (one + two)
        merged = mixed * (one / (one + two))[:, :1] + o_in[t].astype(F32) * share[:, :1]
        merged = merged.astype(BF16)
        for i in range(2):
            n = t * 2 + i
            ab[core, t, xh, :, i * 128 : (i + 1) * 128] = jnp.dot(
                merged[i * 128 : (i + 1) * 128], up_ref[:, 256 * n + 128 : 256 * n + 256], preferred_element_type=F32
            ).astype(BF16)
        a_copy(t, 0).start()
        a_copy(t, 1).start()
        serve(11 + t)
    @pl.when(mine)
    def _():
        for i in (1, 2, 3):
            za_copy(i).wait_send()
            for t in (0, 1):
                zb_copy(i - 1, t).wait_send()

    for f in (0, 1):
        for t in (0, 1):
            for i in (1, 2, 3):
                k1_copy(f, t, i).wait_send()
            for j in range(4):
                k3_copy(f, t, j).wait_send()
                for side in (0, 1):
                    k2_copy(f, t, j, side).wait_send()

    for t in range(2):
        a_wait(t, core, 1 - xh)
        a_copy(t, 2).start()
    for t in range(2):
        a_wait(t, other, xh)
        a_wait(t, other, 1 - xh)

    def p_copy(slot, r):
        dist = (slot + 1) // 2
        zb = (z - dist) % 16 if slot % 2 else (z + dist) % 16
        to = r * 2 + (zb // 4) % 2
        dst, got = across.at[zb // 8, x, zb % 4], p_r.at[zb // 8]
        return (
            to == x,
            remote(stage.at[slot, r], dst, p_s.at[slot, r], got, dev(to, y, z, core)),
            pltpu.make_async_copy(stage.at[slot, r], dst, got),
        )

    def s_copy(g, j, k):
        src, dst = halves.at[g, j, pl.ds(2 * k, 2)], parts.at[y, core]
        return (
            jnp.logical_and(2 * j + g == y, k == core),
            remote(src, dst, s_s.at[g, j, k], s_r, dev(x, 2 * j + g, z, k)),
            pltpu.make_async_copy(src, dst, s_r),
        )

    def launch(copies):
        stays, far, near = copies
        pl.when(jnp.logical_not(stays))(far.start)
        pl.when(stays)(near.start)

    def fold(g):
        remote(across.at[g], across.at[g], p_s.at[0, 0], p_r.at[g], dev(x, y, z, other)).wait_recv()
        for j in range(2):
            halves[g, j] = (across[g, 2 * j].astype(F32) + across[g, 2 * j + 1].astype(F32)).astype(BF16)
            for k in range(2):
                launch(s_copy(g, j, k))

    def project(first, count):
        made = None
        for e in range(2):
            for t in range(2):
                weights = wb[e, t, first : first + count].reshape(count * 112, 256)
                term = dot_nt(weights, ab[e, t].reshape(256, 256))
                made = term if made is None else made + term
        made = made.astype(BF16)
        for i in range(count):
            for r in range(2):
                stage[first + i, r] = made[i * 112 : (i + 1) * 112, r * 128 : (r + 1) * 128]
                launch(p_copy(first + i, r))

    project(0, 4)
    project(4, 5)
    project(9, 4)
    serve(13)
    project(13, 2)
    serve(14)
    project(15, 1)

    for copy in wx:
        copy.wait_send()
    q_copy.wait_send()
    for way in (0, 1):
        for u in range(30):
            w_copy(way, u).wait_send()
    for t in range(2):
        for i in range(2):
            m_copy(t, i).wait_send()
        for i in range(3):
            a_copy(t, i).wait_send()

    near_half = z // 8
    fold(near_half)
    fold(1 - near_half)
    for slot in range(16):
        for r in range(2):
            stays, far, _ = p_copy(slot, r)
            pl.when(jnp.logical_not(stays))(far.wait_send)
    remote(parts, parts, s_s.at[0, 0, 0], s_r, dev(x, y, z, other)).wait_recv()
    for k in range(2):
        for i in range(2):
            result = parts[0, k, i].astype(F32)
            for yy in range(1, 4):
                result = result + parts[yy, k, i].astype(F32)
            out_ref[i * 224 + k * 112 : i * 224 + (k + 1) * 112, :] = result.astype(BF16)

    for g in range(2):
        for j in range(2):
            for k in range(2):
                stays, far, _ = s_copy(g, j, k)
                pl.when(jnp.logical_not(stays))(far.wait_send)


def shards(queries, latents, latent_gain, latent_up, out_weight, positions):
    dma = pltpu.SemaphoreType.DMA
    vmem = pltpu.VMEM
    made = pl.pallas_call(
        kernel,
        out_shape=jax.ShapeDtypeStruct((448, 128), BF16),
        in_specs=[pl.BlockSpec(memory_space=pltpu.HBM)] * 6,
        out_specs=pl.BlockSpec(memory_space=pltpu.VMEM),
        scratch_shapes=[
            vmem((128, 768), BF16),
            vmem((576, 128), BF16),
            vmem((1, 512), F32),
            vmem((512, 1024), BF16),
            vmem((1, 128), jnp.int32),
            vmem((128, WIDE), BF16),
            vmem((2, 4, 4, 64, WIDE), BF16),
            vmem((8, 128, WIDE), BF16),
            vmem((2, 2, 16, 112, 256), BF16),
            vmem((2, 2, 2, 128, 256), BF16),
            vmem((8, 4, 256, 256), F32),
            vmem((128, 128), F32),
            vmem((128, 256), F32),
            vmem((2, 256, 512), BF16),
            vmem((2, 256, 512), BF16),
            vmem((2, 256, 128), F32),
            vmem((2, 256, 128), F32),
            vmem((16, 2, 112, 128), BF16),
            vmem((2, 4, 4, 112, 128), BF16),
            vmem((2, 2, 4, 112, 128), BF16),
            vmem((4, 2, 2, 112, 128), BF16),
            dma((3,)), dma((3,)), dma((3, 2)), dma((2, 2)),
            dma((2, 2, 3)), dma((2, 2, 4, 2)), dma((2, 2, 4)), dma((2, 4, 4, 2)),
            dma((2,)), dma((2,)), dma, dma,
            dma((2, 30)), dma((2, 30)), dma((2, 2)), dma((2, 2)),
            dma((2, 3)), dma((2, 2, 2)), dma((16, 2)), dma((2,)), dma((2, 2, 2)), dma, dma((7,)),
        ],
        compiler_params=pltpu.CompilerParams(
            collective_id=0, has_side_effects=True, vmem_limit_bytes=62 * 1024 * 1024
        ),
        cost_estimate=pl.CostEstimate(flops=8_000_000_000, bytes_accessed=4_000_000, transcendentals=2_200_000),
    )(
        queries, latents.T, latent_gain.reshape(1, 512), latent_up, out_weight.T, positions.reshape(1, 128)
    )
    return made.T


def solution(mesh):
    in_specs = (P("ctx", "head"), P("ctx", None), P(), P(None, "head"), P("head", "ctx"), P("ctx"))
    out_specs = P("ctx", "head")
    return jax.shard_map(shards, mesh=mesh, in_specs=in_specs, out_specs=out_specs, check_vma=False)
```
